32 devices in a mesh: dp: 2 (over x), seq: 16 (over z, y, core).
Axes of the slice: x: 2, y: 2, z: 4, core: 2. Of those that a mesh axis runs over, the one named last changes fastest.
Arguments:
- tokens: bfloat16 [2, 32, 256, 768], P('dp', 'seq'), may hold values from -6 to 6
- upstream: bfloat16 [2, 32, 256, 768], P('dp', 'seq'), may hold values from -0.15625 to 0.15625
- row_factor: bfloat16 [32, 256, 256], P('seq'), may hold values from -0.375 to 0.375
- column_factor: bfloat16 [256, 32, 32], P('seq'), may hold values from -1 to 1
Outputs:
- grad_row: bfloat16 [32, 256, 256], P('seq')
- grad_column: bfloat16 [256, 32, 32], P('seq')
The draws below stay inside these ranges and needn't reach their ends.
All inputs are finite; a program needn't handle non-finite values.
Results may differ from the reference program's by a relative error of at most 0.005.
Values may be sent and summed in bfloat16 or wider, within the bound.
A program may use at most 64 MiB of HBM per device.

```python
import jax
import jax.numpy as jnp
from jax import lax

C = 256
D = 768
R = 32
DOCS = 2


def level_of(stream_key, dims, split, smallest, top_value):
    factor_of, own = 1.0, jax.random.fold_in(stream_key, 6)
    for dim, shards_of in split:
        heights = jnp.exp(jax.random.uniform(jax.random.fold_in(own, dim), (shards_of,), jnp.float32, smallest / len(split), top_value / len(split)))
        factor_of = factor_of * jnp.repeat(heights, dims[dim] // shards_of).reshape([-1 if axis == dim else 1 for axis in range(len(dims))])
    return factor_of


def bell_draw(stream_key, dims, deviation, limit, cuts=(), held_as=jnp.bfloat16):
    result = deviation * jax.random.normal(stream_key, dims, jnp.float32)
    if cuts:
        result = result * level_of(stream_key, dims, cuts, -0.22, 0.18)
    return jnp.clip(result, -limit, limit).astype(held_as)


def setup_inputs(seed: int = 0) -> dict:
    streams_of = jax.random.split(jax.random.key(seed), 5)
    return {
        "tokens": bell_draw(streams_of[0], (DOCS, R, C, D), 1.0, 6.0, ((0, 2), (1, 16))),
        "upstream": bell_draw(streams_of[1], (DOCS, R, C, D), (D * DOCS) ** -0.5, 0.15625, ((0, 2), (1, 16))),
        "row_factor": bell_draw(streams_of[2], (R, C, C), C ** -0.5, 0.375, ((0, 16),)),
        "column_factor": bell_draw(streams_of[3], (C, R, R), R ** -0.5, 1.0, ((0, 16),)),
    }


def reference(tokens, upstream, row_factor, column_factor):
    row_float = row_factor.astype(jnp.float32)
    column_float = column_factor.astype(jnp.float32)
    high = lax.Precision.HIGHEST

    def one_document(carry, pair):
        sum_row, sum_column = carry
        doc_tokens, doc_upstream = pair
        tokens_float = doc_tokens.astype(jnp.float32)
        upstream_float = doc_upstream.astype(jnp.float32)
        mixed = jnp.einsum("rij,rjd->rid", row_float, tokens_float, precision=high).astype(jnp.bfloat16)
        mixed_float = mixed.astype(jnp.float32)
        sum_column = sum_column + jnp.einsum("rcd,scd->crs", upstream_float, mixed_float, precision=high)
        back_mixed = jnp.einsum("crs,rcd->scd", column_float, upstream_float, precision=high).astype(jnp.bfloat16)
        sum_row = sum_row + jnp.einsum("rid,rjd->rij", back_mixed.astype(jnp.float32), tokens_float, precision=high)
        return (sum_row, sum_column), None

    start = (jnp.zeros(row_factor.shape, jnp.float32), jnp.zeros(column_factor.shape, jnp.float32))
    (sum_row, sum_column), unused = lax.scan(one_document, start, (tokens, upstream))
    return sum_row.astype(jnp.bfloat16), sum_column.astype(jnp.bfloat16)
```

```python
import functools

import jax
import jax.numpy as jnp
from jax import lax
from jax.experimental import pallas as pl
from jax.experimental.pallas import tpu as pltpu
from jax.sharding import PartitionSpec as P

F32, BF16 = jnp.float32, jnp.bfloat16


def apply_rows(row_factor, tokens):
    return jnp.einsum(
        "rij,brjd->brid", row_factor, tokens, preferred_element_type=F32
    ).astype(BF16)


def plain_shards(tokens, upstream, row_factor, column_factor):
    mixed = apply_rows(row_factor, tokens)
    mixed_cols, upstream_cols = (
        lax.all_to_all(mixed, "seq", split_axis=2, concat_axis=1, tiled=True),
        lax.all_to_all(upstream, "seq", split_axis=2, concat_axis=1, tiled=True),
    )
    sum_column = jnp.einsum(
        "brcd,bscd->crs", upstream_cols, mixed_cols, preferred_element_type=F32
    )
    back_cols = jnp.einsum(
        "crs,brcd->bscd", column_factor, upstream_cols, preferred_element_type=F32
    ).astype(BF16)
    back_rows = lax.all_to_all(back_cols, "seq", split_axis=1, concat_axis=2, tiled=True)
    sum_row = jnp.einsum("brid,brjd->rij", back_rows, tokens, preferred_element_type=F32)
    total_row, total_column = lax.psum((sum_row, sum_column), "dp")
    return (total_row.astype(BF16), total_column.astype(BF16))


def dot(a, b, ca=1, cb=0):
    return lax.dot_general(a, b, (((ca,), (cb,)), ((), ())), preferred_element_type=F32)


def kernel(n, group, tok, up, rf, cf, grow, gcol,
           U, M, mloc, bloc, B, kmat, prow, precv, pcol, pcolr,
           su, ru, sm, rm, sb, rb, sr, rr, sc, rc):
    me = lax.axis_index("seq")
    other = 1 - lax.axis_index("dp")
    rows, C, D = up.shape
    cols = C // n
    R = rows * n
    lc, lr = cols.bit_length() - 1, R.bit_length() - 1
    full = R * cols
    groups = n // group

    def at(p, width=cols):
        return pl.ds(pl.multiple_of(p * width, width), width)

    def peer_of(k):
        return lax.rem(me + k, n)

    def remote(src, dst, send, recv, p):
        return pltpu.make_async_remote_copy(
            src_ref=src, dst_ref=dst, send_sem=send, recv_sem=recv,
            device_id={"seq": p}, device_id_type=pl.DeviceIdType.MESH)

    def across(src, dst, send, recv):
        return pltpu.make_async_remote_copy(
            src_ref=src, dst_ref=dst, send_sem=send, recv_sem=recv,
            device_id={"dp": other}, device_id_type=pl.DeviceIdType.MESH)

    def each_peer(body):
        @pl.loop(1, n)
        def _(k):
            body(peer_of(k))

    barrier = pltpu.get_barrier_semaphore()
    each_peer(lambda p: pl.semaphore_signal(
        barrier, inc=1, device_id={"seq": p}, device_id_type=pl.DeviceIdType.MESH))
    pl.semaphore_signal(barrier, inc=1, device_id={"dp": other}, device_id_type=pl.DeviceIdType.MESH)
    pl.semaphore_wait(barrier, n)

    each_peer(lambda p: remote(up.at[:, at(p), :], U.at[me], su.at[p], ru.at[me], p).start())
    U[me] = up[:, at(me), :]

    for r in range(rows):
        for h in range(0, D, 256):
            mloc[r, :, h:h + 256] = dot(rf[r], tok[r, :, h:h + 256]).astype(BF16)
    each_peer(lambda p: remote(mloc.at[:, at(p), :], M.at[me], sm.at[p], rm.at[me], p).start())
    M[me] = mloc[:, at(me), :]

    def iota(shape, dim):
        return lax.broadcasted_iota(jnp.int32, shape, dim)

    i, j = iota((full, full), 0), iota((full, full), 1)
    perm = (((i >> lr) == (j & (cols - 1))) & ((i & (R - 1)) == (j >> lc))).astype(F32).astype(BF16)
    spread = ((iota((full, R), 0) >> lc) == iota((full, R), 1)).astype(F32).astype(BF16)
    same = (i & (cols - 1)) == (j & (cols - 1))
    turned = dot(cf[...], perm, 0, 0).astype(BF16)
    kmat[...] = jnp.where(same, dot(spread, turned), 0.0).astype(BF16)

    each_peer(lambda p: remote(up.at[:, at(p), :], U.at[p], su.at[p], ru.at[p], p).wait_recv())
    for h in range(0, D, 256):
        flat = U[:, :, :, h:h + 256].reshape(full, 256)
        bloc[:, :, :, h:h + 256] = dot(kmat[...], flat).astype(BF16).reshape(n, rows, cols, 256)
    each_peer(lambda p: remote(bloc.at[p], B.at[me], sb.at[p], rb.at[me], p).start())
    B[me] = bloc[me]

    each_peer(lambda p: remote(mloc.at[:, at(p), :], M.at[p], sm.at[p], rm.at[p], p).wait_recv())
    pairs = dot(M[...].reshape(full, D), U[...].reshape(full, D), 1, 1)
    pairs = jnp.where(same, pairs, 0.0)
    high = pairs.astype(BF16)
    low = pairs - high.astype(F32)
    mid = low.astype(BF16)
    rest = (low - mid.astype(F32)).astype(BF16)
    pcol[...] = dot(spread, high, 0, 0) + dot(spread, mid, 0, 0) + dot(spread, rest, 0, 0)
    col_copy = across(pcol, pcolr, sc, rc)
    col_copy.start()

    def row_copy(g):
        part = at(g, group * cols)
        return across(prow.at[:, part, :], precv.at[:, part, :], sr.at[g], rr.at[g])

    first = lax.div(me, group)

    @pl.loop(0, groups)
    def _(k):
        g = lax.rem(first + k, groups)

        @pl.loop(0, group)
        def _(q):
            p = g * group + q

            @pl.when(p != me)
            def _():
                remote(bloc.at[p], B.at[p], sb.at[p], rb.at[p], p).wait_recv()

        part = at(g, group * cols)
        for r in range(rows):
            block = B[pl.ds(g * group, group), r].reshape(group * cols, D)
            prow[r, part, :] = dot(block, tok[r], 1, 1)
        row_copy(g).start()

    col_copy.wait()
    total = (pcol[...] + pcolr[...]).astype(BF16)
    gcol[...] = dot(perm, total, 1, 1).astype(BF16)

    @pl.loop(0, groups)
    def _(k):
        g = lax.rem(first + k, groups)
        row_copy(g).wait()
        part = at(g, group * cols)
        grow[:, part, :] = (prow[:, part, :] + precv[:, part, :]).astype(BF16)

    def finish(p):
        remote(up.at[:, at(p), :], U.at[me], su.at[p], ru.at[me], p).wait_send()
        remote(mloc.at[:, at(p), :], M.at[me], sm.at[p], rm.at[me], p).wait_send()
        remote(bloc.at[p], B.at[me], sb.at[p], rb.at[me], p).wait_send()

    each_peer(finish)


def fused_shards(n, tokens, upstream, row_factor, column_factor):
    _, rows, C, D = tokens.shape
    cols, R = C // n, rows * n
    full = R * cols
    group = 4
    groups = n // group
    vmem = pl.BlockSpec(memory_space=pltpu.VMEM)
    dma = pltpu.SemaphoreType.DMA
    grow, gcol = pl.pallas_call(
        functools.partial(kernel, n, group),
        out_shape=(
            jax.ShapeDtypeStruct((rows, C, C), BF16),
            jax.ShapeDtypeStruct((full, R), BF16),
        ),
        in_specs=[vmem] * 4,
        out_specs=(vmem, vmem),
        scratch_shapes=[
            pltpu.VMEM((n, rows, cols, D), BF16),
            pltpu.VMEM((n, rows, cols, D), BF16),
            pltpu.VMEM((rows, C, D), BF16),
            pltpu.VMEM((n, rows, cols, D), BF16),
            pltpu.VMEM((n, rows, cols, D), BF16),
            pltpu.VMEM((full, full), BF16),
            pltpu.VMEM((rows, C, C), F32),
            pltpu.VMEM((rows, C, C), F32),
            pltpu.VMEM((R, full), F32),
            pltpu.VMEM((R, full), F32),
        ] + [dma((n,))] * 6 + [dma((groups,))] * 2 + [dma, dma],
        compiler_params=pltpu.CompilerParams(
            collective_id=0, has_side_effects=True, vmem_limit_bytes=40 << 20
        ),
    )(tokens[0], upstream[0], row_factor, column_factor.reshape(full, R))
    return grow, gcol.reshape(cols, R, R)


def shards(n, m, tokens, upstream, row_factor, column_factor):
    docs, rows, C, D = tokens.shape
    cols, R = C // n, rows * n
    power = R & (R - 1) == 0 and cols & (cols - 1) == 0
    if m == 2 and docs == 1 and n % 4 == 0 and cols % 16 == 0 and D % 256 == 0 and power:
        return fused_shards(n, tokens, upstream, row_factor, column_factor)
    return plain_shards(tokens, upstream, row_factor, column_factor)


def solution(mesh):
    placed = (
        P("dp", "seq", None, None),
        P("dp", "seq", None, None),
        P("seq", None, None),
        P("seq", None, None),
    )
    return jax.shard_map(
        functools.partial(shards, mesh.shape["seq"], mesh.shape["dp"]),
        mesh=mesh,
        in_specs=placed,
        out_specs=(P("seq", None, None), P("seq", None, None)),
        check_vma=False,
    )
```

```python
import functools

import jax
import jax.numpy as jnp
from jax import lax
from jax.experimental import pallas as pl
from jax.experimental.pallas import tpu as pltpu
from jax.sharding import PartitionSpec as P

F32, BF16 = jnp.float32, jnp.bfloat16


def apply_rows(row_factor, tokens):
    return jnp.einsum(
        "rij,brjd->brid", row_factor, tokens, preferred_element_type=F32
    ).astype(BF16)


def plain_shards(tokens, upstream, row_factor, column_factor):
    mixed = apply_rows(row_factor, tokens)
    mixed_cols, upstream_cols = (
        lax.all_to_all(mixed, "seq", split_axis=2, concat_axis=1, tiled=True),
        lax.all_to_all(upstream, "seq", split_axis=2, concat_axis=1, tiled=True),
    )
    sum_column = jnp.einsum(
        "brcd,bscd->crs", upstream_cols, mixed_cols, preferred_element_type=F32
    )
    back_cols = jnp.einsum(
        "crs,brcd->bscd", column_factor, upstream_cols, preferred_element_type=F32
    ).astype(BF16)
    back_rows = lax.all_to_all(back_cols, "seq", split_axis=1, concat_axis=2, tiled=True)
    sum_row = jnp.einsum("brid,brjd->rij", back_rows, tokens, preferred_element_type=F32)
    total_row, total_column = lax.psum((sum_row, sum_column), "dp")
    return (total_row.astype(BF16), total_column.astype(BF16))


def dot(a, b, ca=1, cb=0):
    return lax.dot_general(a, b, (((ca,), (cb,)), ((), ())), preferred_element_type=F32)


def kernel(n, outer_jobs, tok, up, rf, cf, grow, gcol,
           U, M, mloc, bloc, B, cfs, prow, precv, pcol, pcolr,
           su, ru, sf, sm, rm, sb, rb, sk, rk, sr, rr, sc, rc):
    me, doc = lax.axis_index("seq"), lax.axis_index("dp")
    other = 1 - doc
    rows, C, D = up.shape
    cols = C // n
    R = rows * n
    lc, lr = cols.bit_length() - 1, R.bit_length() - 1
    full, part_rows = R * cols, R * cols // 2
    layers, plane, half_n = 4, n // 4, n // 2
    inner_jobs = layers - outer_jobs
    half = lax.div(me, half_n)
    layer = lax.div(me, plane)
    outer = (layer == 0) | (layer == layers - 1)
    jobs = jnp.where(outer, outer_jobs, inner_jobs)
    first_k = jnp.where(outer, 0, outer_jobs)
    base = half * half_n
    MESH = pl.DeviceIdType.MESH

    def at(p, width=cols):
        return pl.ds(pl.multiple_of(p * width, width), width)

    def owner(h, j):
        k, place = lax.div(j, plane), lax.rem(j, plane)
        far = k < outer_jobs
        z = jnp.where(far, h * (layers - 1), 1 + h)
        return z * plane + place, jnp.where(far, k, k - outer_jobs)

    def chunk(slot):
        return (first_k + slot) * plane + lax.rem(me, plane)

    def remote(src, dst, send, recv, p, d=None):
        return pltpu.make_async_remote_copy(
            src_ref=src, dst_ref=dst, send_sem=send, recv_sem=recv,
            device_id={"dp": doc if d is None else d, "seq": p}, device_id_type=MESH)

    def greet(p, d):
        pl.semaphore_signal(barrier, inc=1, device_id={"dp": d, "seq": p}, device_id_type=MESH)

    barrier = pltpu.get_barrier_semaphore()

    @pl.loop(1, n)
    def _(k):
        greet(lax.rem(me + k, n), doc)

    greet(me, other)

    @pl.loop(0, jobs)
    def _(slot):
        greet(chunk(slot), other)

    for h in range(2):
        greet(owner(h, me)[0], other)
    pl.semaphore_wait(barrier, n + 2 + jobs)

    def u_copy(h, j):
        p, slot = owner(h, j)
        return p, remote(up.at[:, at(j), :], U.at[slot, me], su.at[h, j], ru.at[slot, me], p)

    def direct(h, j):
        return (h == half) | jnp.logical_not(outer) | (lax.div(j, plane) < outer_jobs)

    def f_copy(h):
        p, slot = owner(h, me)
        return p, remote(cf, cfs.at[slot], sk.at[h], rk.at[slot], p)

    @pl.loop(0, n)
    def _(j):
        for far in (1, 0):
            h = 1 - half if far else half
            p, copy = u_copy(h, j)

            @pl.when((p != me) & direct(h, j))
            def _():
                copy.start()

    for h in range(2):
        p, copy = f_copy(h)

        @pl.when(p != me)
        def _():
            copy.start()

        @pl.when(p == me)
        def _():
            cfs[owner(h, me)[1]] = cf[...]

    @pl.loop(0, jobs)
    def _(slot):
        U[slot, me] = up[:, at(chunk(slot)), :]

    for r in range(rows):
        for q in range(0, D, 256):
            mloc[r, :, q:q + 256] = dot(rf[r], tok[r, :, q:q + 256]).astype(BF16)

    def wait_u_sends():
        @pl.loop(0, n)
        def _(j):
            for h in range(2):
                p, copy = u_copy(h, j)

                @pl.when((p != me) & direct(h, j))
                def _():
                    copy.wait_send()

    @pl.when(outer)
    def _():
        wait_u_sends()

    def m_copy(j):
        p, slot = owner(half, j)
        src = me - base
        return p, remote(mloc.at[:, at(j), :], M.at[slot, src], sm.at[j], rm.at[slot, src], p)

    @pl.loop(0, n)
    def _(j):
        p, copy = m_copy(j)

        @pl.when(p != me)
        def _():
            copy.start()

    @pl.loop(0, jobs)
    def _(slot):
        M[slot, me - base] = mloc[:, at(chunk(slot)), :]

    def u_arrival(slot, src):
        return remote(U.at[slot, src], U.at[slot, src], sf.at[slot, lax.rem(src, plane)],
                      ru.at[slot, src], n - 1 - me + 2 * lax.rem(me, plane) - plane + 1)

    edge = half * (layers - 1) * plane

    @pl.when(jnp.logical_not(outer))
    def _():
        @pl.loop(0, inner_jobs)
        def _(slot):
            @pl.loop(0, plane)
            def _(q):
                copy = u_arrival(slot, edge + q)
                copy.wait_recv()
                copy.start()

    def iota(shape, dim):
        return lax.broadcasted_iota(jnp.int32, shape, dim)

    def ones(mask):
        return mask.astype(F32).astype(BF16)

    i, j = iota((full, full), 0), iota((full, full), 1)
    perm = ones(((i >> lr) == (j & (cols - 1))) & ((i & (R - 1)) == (j >> lc)))
    same = (iota((part_rows, full), 0) & (cols - 1)) == (iota((part_rows, full), 1) & (cols - 1))
    spread = ones((iota((part_rows, R), 0) >> lc) + half * (R // 2) == iota((part_rows, R), 1))
    gather = ones((iota((part_rows, R // 2), 0) >> lc) == iota((part_rows, R // 2), 1))

    def b_copy(slot, q):
        j = chunk(slot)
        return base + q, remote(bloc.at[slot, q], B.at[j], sb.at[slot, q], rb.at[j], base + q)

    def back(slot):
        @pl.when(slot < jobs)
        def _():
            j = chunk(slot)

            @pl.when((j != me))
            def _():
                remote(cf, cfs.at[slot], sk.at[0], rk.at[slot], lax.rem(me + 1, n)).wait_recv()

            turned = dot(cfs[slot], perm, 0, 0).astype(BF16)
            kmat = jnp.where(same, dot(spread, turned), 0.0).astype(BF16)

            @pl.loop(0, n)
            def _(src):
                handed = jnp.logical_not(outer) & (src >= edge) & (src < edge + plane)

                @pl.when((src != me) & jnp.logical_not(handed))
                def _():
                    u_arrival(slot, src).wait_recv()

            for q in range(0, D, 256):
                flat = U[slot, :, :, :, q:q + 256].reshape(full, 256)
                bloc[slot, :, :, :, q:q + 256] = dot(kmat, flat).astype(BF16).reshape(
                    half_n, rows, cols, 256)

            @pl.loop(0, half_n)
            def _(q):
                p, copy = b_copy(slot, q)

                @pl.when(p != me)
                def _():
                    copy.start()

            B[j] = bloc[slot, me - base]

    def s_copy(slot, d):
        return remote(pcol.at[slot], pcolr.at[half, doc], sc.at[slot, d], rc.at[half, doc],
                      chunk(slot), d)

    def here(slot, d):
        return (chunk(slot) == me) & (doc == d)

    def column(slot):
        @pl.when(slot < jobs)
        def _():
            @pl.loop(0, half_n)
            def _(src):
                @pl.when(base + src != me)
                def _():
                    remote(mloc.at[:, at(0), :], M.at[slot, src], sm.at[0], rm.at[slot, src],
                           lax.rem(me + 1, n)).wait_recv()

            pairs = dot(M[slot].reshape(part_rows, D), U[slot].reshape(full, D), 1, 1)
            pairs = jnp.where(same, pairs, 0.0)
            high = pairs.astype(BF16)
            low = pairs - high.astype(F32)
            mid = low.astype(BF16)
            rest = (low - mid.astype(F32)).astype(BF16)
            pcol[slot] = dot(gather, high, 0, 0) + dot(gather, mid, 0, 0) + dot(gather, rest, 0, 0)
            for d in range(2):
                @pl.when(jnp.logical_not(here(slot, d)))
                def _():
                    s_copy(slot, d).start()

                @pl.when(here(slot, d))
                def _():
                    pcolr[half, doc] = pcol[slot]

    def row_copy(k):
        part = at(k, plane * cols)
        return remote(prow.at[:, part, :], precv.at[:, part, :], sr.at[k], rr.at[k], me, other)

    def row(k):
        @pl.loop(0, plane)
        def _(q):
            j = k * plane + q
            p, _slot = owner(half, j)

            @pl.when(p != me)
            def _():
                remote(bloc.at[0, 0], B.at[j], sb.at[0, 0], rb.at[j], p).wait_recv()

        part = at(k, plane * cols)
        for r in range(rows):
            block = B[k * plane:(k + 1) * plane, r].reshape(plane * cols, D)
            prow[r, part, :] = dot(block, tok[r], 1, 1)
        row_copy(k).start()

    back(0)
    back(1)
    row(0)
    back(2)
    row(1)
    column(0)
    column(1)
    column(2)
    row(2)
    row(3)

    for h in range(2):
        for d in range(2):
            p, _slot = owner(h, me)

            @pl.when(jnp.logical_not((p == me) & (doc == d)))
            def _():
                remote(pcol.at[0], pcolr.at[h, d], sc.at[0, 0], rc.at[h, d],
                       lax.rem(me + 1, n)).wait_recv()

    total = jnp.concatenate([pcolr[0, 0] + pcolr[0, 1], pcolr[1, 0] + pcolr[1, 1]], axis=0)
    gcol[...] = dot(perm, total.astype(BF16), 1, 1).astype(BF16)

    for k in range(layers):
        row_copy(k).wait()
        part = pl.ds(k * plane * cols, plane * cols)
        grow[:, part, :] = (prow[:, part, :] + precv[:, part, :]).astype(BF16)

    @pl.when(jnp.logical_not(outer))
    def _():
        wait_u_sends()

        @pl.loop(0, inner_jobs)
        def _(slot):
            @pl.loop(0, plane)
            def _(q):
                u_arrival(slot, edge + q).wait_send()

    for h in range(2):
        p, copy = f_copy(h)

        @pl.when(p != me)
        def _():
            copy.wait_send()

    @pl.loop(0, n)
    def _(j):
        p, copy = m_copy(j)

        @pl.when(p != me)
        def _():
            copy.wait_send()

    @pl.loop(0, jobs)
    def _(slot):
        @pl.loop(0, half_n)
        def _(q):
            p, copy = b_copy(slot, q)

            @pl.when(p != me)
            def _():
                copy.wait_send()

        for d in range(2):
            @pl.when(jnp.logical_not(here(slot, d)))
            def _():
                s_copy(slot, d).wait_send()


def fused_shards(n, tokens, upstream, row_factor, column_factor):
    _, rows, C, D = tokens.shape
    cols, R = C // n, rows * n
    full = R * cols
    outer_jobs, slots = 1, 3
    vmem = pl.BlockSpec(memory_space=pltpu.VMEM)
    dma = pltpu.SemaphoreType.DMA
    grow, gcol = pl.pallas_call(
        functools.partial(kernel, n, outer_jobs),
        out_shape=(
            jax.ShapeDtypeStruct((rows, C, C), BF16),
            jax.ShapeDtypeStruct((full, R), BF16),
        ),
        in_specs=[vmem] * 4,
        out_specs=(vmem, vmem),
        scratch_shapes=[
            pltpu.VMEM((slots, n, rows, cols, D), BF16),
            pltpu.VMEM((slots, n // 2, rows, cols, D), BF16),
            pltpu.VMEM((rows, C, D), BF16),
            pltpu.VMEM((slots, n // 2, rows, cols, D), BF16),
            pltpu.VMEM((n, rows, cols, D), BF16),
            pltpu.VMEM((slots, full, R), BF16),
            pltpu.VMEM((rows, C, C), F32),
            pltpu.VMEM((rows, C, C), F32),
            pltpu.VMEM((slots, R // 2, full), F32),
            pltpu.VMEM((2, 2, R // 2, full), F32),
            dma((2, n)), dma((slots, n)), dma((slots, n // 4)),
            dma((n,)), dma((slots, n // 2)),
            dma((slots, n // 2)), dma((n,)),
            dma((2,)), dma((slots,)),
            dma((4,)), dma((4,)),
            dma((slots, 2)), dma((2, 2)),
        ],
        compiler_params=pltpu.CompilerParams(
            collective_id=0, has_side_effects=True, vmem_limit_bytes=48 << 20
        ),
    )(tokens[0], upstream[0], row_factor, column_factor.reshape(full, R))
    return grow, gcol.reshape(cols, R, R)


def shards(n, m, tokens, upstream, row_factor, column_factor):
    docs, rows, C, D = tokens.shape
    cols, R = C // n, rows * n
    power = R & (R - 1) == 0 and cols & (cols - 1) == 0
    if m == 2 and docs == 1 and n == 16 and cols % 16 == 0 and D % 256 == 0 and power:
        return fused_shards(n, tokens, upstream, row_factor, column_factor)
    return plain_shards(tokens, upstream, row_factor, column_factor)


def solution(mesh):
    placed = (
        P("dp", "seq", None, None),
        P("dp", "seq", None, None),
        P("seq", None, None),
        P("seq", None, None),
    )
    return jax.shard_map(
        functools.partial(shards, mesh.shape["seq"], mesh.shape["dp"]),
        mesh=mesh,
        in_specs=placed,
        out_specs=(P("seq", None, None), P("seq", None, None)),
        check_vma=False,
    )
```

```python
import functools

import jax
import jax.numpy as jnp
from jax import lax
from jax.experimental import pallas as pl
from jax.experimental.pallas import tpu as pltpu
from jax.sharding import PartitionSpec as P

F32, BF16 = jnp.float32, jnp.bfloat16


def apply_rows(row_factor, tokens):
    return jnp.einsum(
        "rij,brjd->brid", row_factor, tokens, preferred_element_type=F32
    ).astype(BF16)


def plain_shards(tokens, upstream, row_factor, column_factor):
    mixed = apply_rows(row_factor, tokens)
    mixed_cols, upstream_cols = (
        lax.all_to_all(mixed, "seq", split_axis=2, concat_axis=1, tiled=True),
        lax.all_to_all(upstream, "seq", split_axis=2, concat_axis=1, tiled=True),
    )
    sum_column = jnp.einsum(
        "brcd,bscd->crs", upstream_cols, mixed_cols, preferred_element_type=F32
    )
    back_cols = jnp.einsum(
        "crs,brcd->bscd", column_factor, upstream_cols, preferred_element_type=F32
    ).astype(BF16)
    back_rows = lax.all_to_all(back_cols, "seq", split_axis=1, concat_axis=2, tiled=True)
    sum_row = jnp.einsum("brid,brjd->rij", back_rows, tokens, preferred_element_type=F32)
    total_row, total_column = lax.psum((sum_row, sum_column), "dp")
    return (total_row.astype(BF16), total_column.astype(BF16))


def dot(a, b, ca=1, cb=0):
    return lax.dot_general(a, b, (((ca,), (cb,)), ((), ())), preferred_element_type=F32)


def kernel(n, outer_jobs, tok, up, rf, cf, grow, gcol,
           U, M, mloc, bloc, B, cfs, prow, precv, pcol, pcolr,
           su, ru, sf, sm, rm, sb, rb, sk, rk, sr, rr, sc, rc):
    me, doc = lax.axis_index("seq"), lax.axis_index("dp")
    other = 1 - doc
    rows, C, D = up.shape
    cols = C // n
    R = rows * n
    lc, lr = cols.bit_length() - 1, R.bit_length() - 1
    full, part_rows = R * cols, R * cols // 2
    layers, plane, half_n = 4, n // 4, n // 2
    inner_jobs = layers - outer_jobs
    half = lax.div(me, half_n)
    layer = lax.div(me, plane)
    outer = (layer == 0) | (layer == layers - 1)
    jobs = jnp.where(outer, outer_jobs, inner_jobs)
    first_k = jnp.where(outer, 0, outer_jobs)
    base = half * half_n
    MESH = pl.DeviceIdType.MESH

    def at(p, width=cols):
        return pl.ds(pl.multiple_of(p * width, width), width)

    def owner(h, j):
        k, place = lax.div(j, plane), lax.rem(j, plane)
        far = k < outer_jobs
        z = jnp.where(far, h * (layers - 1), 1 + h)
        return z * plane + place, jnp.where(far, k, k - outer_jobs)

    def chunk(slot):
        return (first_k + slot) * plane + lax.rem(me, plane)

    def remote(src, dst, send, recv, p, d=None):
        return pltpu.make_async_remote_copy(
            src_ref=src, dst_ref=dst, send_sem=send, recv_sem=recv,
            device_id={"dp": doc if d is None else d, "seq": p}, device_id_type=MESH)

    def greet(p, d):
        pl.semaphore_signal(barrier, inc=1, device_id={"dp": d, "seq": p}, device_id_type=MESH)

    barrier = pltpu.get_barrier_semaphore()

    @pl.loop(1, n)
    def _(k):
        greet(lax.rem(me + k, n), doc)

    greet(me, other)

    @pl.loop(0, jobs)
    def _(slot):
        greet(chunk(slot), other)

    for h in range(2):
        greet(owner(h, me)[0], other)
    pl.semaphore_wait(barrier, n + 2 + jobs)

    def u_copy(h, j):
        p, slot = owner(h, j)
        return p, remote(up.at[:, at(j), :], U.at[slot, me], su.at[h, j], ru.at[slot, me], p)

    def direct(h, j):
        return (h == half) | jnp.logical_not(outer) | (lax.div(j, plane) < outer_jobs)

    def f_copy(h):
        p, slot = owner(h, me)
        return p, remote(cf, cfs.at[slot], sk.at[h], rk.at[slot], p)

    @pl.loop(0, n)
    def _(j):
        for far in (1, 0):
            h = 1 - half if far else half
            p, copy = u_copy(h, j)

            @pl.when((p != me) & direct(h, j))
            def _():
                copy.start()

    for h in range(2):
        p, copy = f_copy(h)

        @pl.when(p != me)
        def _():
            copy.start()

        @pl.when(p == me)
        def _():
            cfs[owner(h, me)[1]] = cf[...]

    @pl.loop(0, jobs)
    def _(slot):
        U[slot, me] = up[:, at(chunk(slot)), :]

    for r in range(rows):
        for q in range(0, D, 256):
            mloc[r, :, q:q + 256] = dot(rf[r], tok[r, :, q:q + 256]).astype(BF16)

    def wait_u_sends():
        @pl.loop(0, n)
        def _(j):
            for h in range(2):
                p, copy = u_copy(h, j)

                @pl.when((p != me) & direct(h, j))
                def _():
                    copy.wait_send()

    @pl.when(outer)
    def _():
        wait_u_sends()

    def m_copy(j):
        p, slot = owner(half, j)
        src = me - base
        return p, remote(mloc.at[:, at(j), :], M.at[slot, src], sm.at[j], rm.at[slot, src], p)

    @pl.loop(0, n)
    def _(j):
        p, copy = m_copy(j)

        @pl.when(p != me)
        def _():
            copy.start()

    @pl.loop(0, jobs)
    def _(slot):
        M[slot, me - base] = mloc[:, at(chunk(slot)), :]

    def u_arrival(slot, src):
        return remote(U.at[slot, src], U.at[slot, src], sf.at[slot, lax.rem(src, plane)],
                      ru.at[slot, src], n - 1 - me + 2 * lax.rem(me, plane) - plane + 1)

    edge = half * (layers - 1) * plane

    @pl.when(jnp.logical_not(outer))
    def _():
        @pl.loop(0, inner_jobs)
        def _(slot):
            @pl.loop(0, plane)
            def _(q):
                copy = u_arrival(slot, edge + q)
                copy.wait_recv()
                copy.start()

    def iota(shape, dim):
        return lax.broadcasted_iota(jnp.int32, shape, dim)

    def ones(mask):
        return mask.astype(F32).astype(BF16)

    i, j = iota((full, full), 0), iota((full, full), 1)
    perm = ones(((i >> lr) == (j & (cols - 1))) & ((i & (R - 1)) == (j >> lc)))
    same = (iota((part_rows, full), 0) & (cols - 1)) == (iota((part_rows, full), 1) & (cols - 1))
    spread = ones((iota((part_rows, R), 0) >> lc) + half * (R // 2) == iota((part_rows, R), 1))
    gather = ones((iota((part_rows, R // 2), 0) >> lc) == iota((part_rows, R // 2), 1))

    def b_copy(slot, q):
        j = chunk(slot)
        return base + q, remote(bloc.at[slot, q], B.at[j], sb.at[slot, q], rb.at[j], base + q)

    def back(slot):
        @pl.when(slot < jobs)
        def _():
            j = chunk(slot)

            @pl.when((j != me))
            def _():
                remote(cf, cfs.at[slot], sk.at[0], rk.at[slot], lax.rem(me + 1, n)).wait_recv()

            turned = dot(cfs[slot], perm, 0, 0).astype(BF16)
            kmat = jnp.where(same, dot(spread, turned), 0.0).astype(BF16)

            @pl.loop(0, n)
            def _(src):
                handed = jnp.logical_not(outer) & (src >= edge) & (src < edge + plane)

                @pl.when((src != me) & jnp.logical_not(handed))
                def _():
                    u_arrival(slot, src).wait_recv()

            for q in range(0, D, 256):
                flat = U[slot, :, :, :, q:q + 256].reshape(full, 256)
                bloc[slot, :, :, :, q:q + 256] = dot(kmat, flat).astype(BF16).reshape(
                    half_n, rows, cols, 256)

            @pl.loop(0, half_n)
            def _(q):
                p, copy = b_copy(slot, q)

                @pl.when(p != me)
                def _():
                    copy.start()

            B[j] = bloc[slot, me - base]

    def s_copy(slot, d):
        return remote(pcol.at[slot], pcolr.at[half, doc], sc.at[slot, d], rc.at[half, doc],
                      chunk(slot), d)

    def here(slot, d):
        return (chunk(slot) == me) & (doc == d)

    def column(slot):
        @pl.when(slot < jobs)
        def _():
            @pl.loop(0, half_n)
            def _(src):
                @pl.when(base + src != me)
                def _():
                    remote(mloc.at[:, at(0), :], M.at[slot, src], sm.at[0], rm.at[slot, src],
                           lax.rem(me + 1, n)).wait_recv()

            pairs = dot(M[slot].reshape(part_rows, D), U[slot].reshape(full, D), 1, 1)
            pairs = jnp.where(same, pairs, 0.0)
            high = pairs.astype(BF16)
            low = pairs - high.astype(F32)
            mid = low.astype(BF16)
            rest = (low - mid.astype(F32)).astype(BF16)
            pcol[slot] = dot(gather, high, 0, 0) + dot(gather, mid, 0, 0) + dot(gather, rest, 0, 0)
            for d in range(2):
                @pl.when(jnp.logical_not(here(slot, d)))
                def _():
                    s_copy(slot, d).start()

                @pl.when(here(slot, d))
                def _():
                    pcolr[half, doc] = pcol[slot]

    def row_copy(k):
        part = at(k, plane * cols)
        return remote(prow.at[:, part, :], precv.at[:, part, :], sr.at[k], rr.at[k], me, other)

    def row(k):
        @pl.loop(0, plane)
        def _(q):
            j = k * plane + q
            p, _slot = owner(half, j)

            @pl.when(p != me)
            def _():
                remote(bloc.at[0, 0], B.at[j], sb.at[0, 0], rb.at[j], p).wait_recv()

        part = at(k, plane * cols)
        for r in range(rows):
            block = B[k * plane:(k + 1) * plane, r].reshape(plane * cols, D)
            prow[r, part, :] = dot(block, tok[r], 1, 1).astype(BF16)
        row_copy(k).start()

    back(0)
    back(1)
    row(0)
    back(2)
    row(1)
    column(0)
    column(1)
    column(2)
    row(2)
    row(3)

    for h in range(2):
        for d in range(2):
            p, _slot = owner(h, me)

            @pl.when(jnp.logical_not((p == me) & (doc == d)))
            def _():
                remote(pcol.at[0], pcolr.at[h, d], sc.at[0, 0], rc.at[h, d],
                       lax.rem(me + 1, n)).wait_recv()

    total = jnp.concatenate([pcolr[0, 0] + pcolr[0, 1], pcolr[1, 0] + pcolr[1, 1]], axis=0)
    gcol[...] = dot(perm, total.astype(BF16), 1, 1).astype(BF16)

    for k in range(layers):
        row_copy(k).wait()
        part = pl.ds(k * plane * cols, plane * cols)
        grow[:, part, :] = (prow[:, part, :].astype(F32) + precv[:, part, :].astype(F32)).astype(BF16)

    @pl.when(jnp.logical_not(outer))
    def _():
        wait_u_sends()

        @pl.loop(0, inner_jobs)
        def _(slot):
            @pl.loop(0, plane)
            def _(q):
                u_arrival(slot, edge + q).wait_send()

    for h in range(2):
        p, copy = f_copy(h)

        @pl.when(p != me)
        def _():
            copy.wait_send()

    @pl.loop(0, n)
    def _(j):
        p, copy = m_copy(j)

        @pl.when(p != me)
        def _():
            copy.wait_send()

    @pl.loop(0, jobs)
    def _(slot):
        @pl.loop(0, half_n)
        def _(q):
            p, copy = b_copy(slot, q)

            @pl.when(p != me)
            def _():
                copy.wait_send()

        for d in range(2):
            @pl.when(jnp.logical_not(here(slot, d)))
            def _():
                s_copy(slot, d).wait_send()


def fused_shards(n, tokens, upstream, row_factor, column_factor):
    _, rows, C, D = tokens.shape
    cols, R = C // n, rows * n
    full = R * cols
    outer_jobs, slots = 1, 3
    vmem = pl.BlockSpec(memory_space=pltpu.VMEM)
    dma = pltpu.SemaphoreType.DMA
    grow, gcol = pl.pallas_call(
        functools.partial(kernel, n, outer_jobs),
        out_shape=(
            jax.ShapeDtypeStruct((rows, C, C), BF16),
            jax.ShapeDtypeStruct((full, R), BF16),
        ),
        in_specs=[vmem] * 4,
        out_specs=(vmem, vmem),
        scratch_shapes=[
            pltpu.VMEM((slots, n, rows, cols, D), BF16),
            pltpu.VMEM((slots, n // 2, rows, cols, D), BF16),
            pltpu.VMEM((rows, C, D), BF16),
            pltpu.VMEM((slots, n // 2, rows, cols, D), BF16),
            pltpu.VMEM((n, rows, cols, D), BF16),
            pltpu.VMEM((slots, full, R), BF16),
            pltpu.VMEM((rows, C, C), BF16),
            pltpu.VMEM((rows, C, C), BF16),
            pltpu.VMEM((slots, R // 2, full), F32),
            pltpu.VMEM((2, 2, R // 2, full), F32),
            dma((2, n)), dma((slots, n)), dma((slots, n // 4)),
            dma((n,)), dma((slots, n // 2)),
            dma((slots, n // 2)), dma((n,)),
            dma((2,)), dma((slots,)),
            dma((4,)), dma((4,)),
            dma((slots, 2)), dma((2, 2)),
        ],
        compiler_params=pltpu.CompilerParams(
            collective_id=0, has_side_effects=True, vmem_limit_bytes=48 << 20
        ),
    )(tokens[0], upstream[0], row_factor, column_factor.reshape(full, R))
    return grow, gcol.reshape(cols, R, R)


def shards(n, m, tokens, upstream, row_factor, column_factor):
    docs, rows, C, D = tokens.shape
    cols, R = C // n, rows * n
    power = R & (R - 1) == 0 and cols & (cols - 1) == 0
    if m == 2 and docs == 1 and n == 16 and cols % 16 == 0 and D % 256 == 0 and power:
        return fused_shards(n, tokens, upstream, row_factor, column_factor)
    return plain_shards(tokens, upstream, row_factor, column_factor)


def solution(mesh):
    placed = (
        P("dp", "seq", None, None),
        P("dp", "seq", None, None),
        P("seq", None, None),
        P("seq", None, None),
    )
    return jax.shard_map(
        functools.partial(shards, mesh.shape["seq"], mesh.shape["dp"]),
        mesh=mesh,
        in_specs=placed,
        out_specs=(P("seq", None, None), P("seq", None, None)),
        check_vma=False,
    )
```

```python
import functools

import jax
import jax.numpy as jnp
from jax import lax
from jax.experimental import pallas as pl
from jax.experimental.pallas import tpu as pltpu
from jax.sharding import PartitionSpec as P

F32, BF16 = jnp.float32, jnp.bfloat16


def apply_rows(row_factor, tokens):
    return jnp.einsum(
        "rij,brjd->brid", row_factor, tokens, preferred_element_type=F32
    ).astype(BF16)


def plain_shards(tokens, upstream, row_factor, column_factor):
    mixed = apply_rows(row_factor, tokens)
    mixed_cols, upstream_cols = (
        lax.all_to_all(mixed, "seq", split_axis=2, concat_axis=1, tiled=True),
        lax.all_to_all(upstream, "seq", split_axis=2, concat_axis=1, tiled=True),
    )
    sum_column = jnp.einsum(
        "brcd,bscd->crs", upstream_cols, mixed_cols, preferred_element_type=F32
    )
    back_cols = jnp.einsum(
        "crs,brcd->bscd", column_factor, upstream_cols, preferred_element_type=F32
    ).astype(BF16)
    back_rows = lax.all_to_all(back_cols, "seq", split_axis=1, concat_axis=2, tiled=True)
    sum_row = jnp.einsum("brid,brjd->rij", back_rows, tokens, preferred_element_type=F32)
    total_row, total_column = lax.psum((sum_row, sum_column), "dp")
    return (total_row.astype(BF16), total_column.astype(BF16))


def dot(a, b, ca=1, cb=0):
    return lax.dot_general(a, b, (((ca,), (cb,)), ((), ())), preferred_element_type=F32)


def kernel(n, outer_jobs, tok, up, rf, cf, grow, gcol,
           U, M, mloc, bloc, B, cfs, prow, precv, pcol, pcolr,
           su, ru, sf, sm, rm, sb, rb, sk, rk, sr, rr, sc, rc):
    me, doc = lax.axis_index("seq"), lax.axis_index("dp")
    other = 1 - doc
    rows, C, D = up.shape
    cols = C // n
    R = rows * n
    lc, lr = cols.bit_length() - 1, R.bit_length() - 1
    full, part_rows = R * cols, R * cols // 2
    layers, plane, half_n = 4, n // 4, n // 2
    inner_jobs = layers - outer_jobs
    half = lax.div(me, half_n)
    layer = lax.div(me, plane)
    outer = (layer == 0) | (layer == layers - 1)
    jobs = jnp.where(outer, outer_jobs, inner_jobs)
    first_k = jnp.where(outer, 0, outer_jobs)
    base = half * half_n
    MESH = pl.DeviceIdType.MESH

    def at(p, width=cols):
        return pl.ds(pl.multiple_of(p * width, width), width)

    def owner(h, j):
        k, place = lax.div(j, plane), lax.rem(j, plane)
        far = k < outer_jobs
        z = jnp.where(far, h * (layers - 1), 1 + h)
        return z * plane + place, jnp.where(far, k, k - outer_jobs)

    def chunk(slot):
        return (first_k + slot) * plane + lax.rem(me, plane)

    def turn(step):
        return lax.div(step, plane) * plane + lax.rem(me + step, plane)

    def remote(src, dst, send, recv, p, d=None):
        return pltpu.make_async_remote_copy(
            src_ref=src, dst_ref=dst, send_sem=send, recv_sem=recv,
            device_id={"dp": doc if d is None else d, "seq": p}, device_id_type=MESH)

    def greet(p, d):
        pl.semaphore_signal(barrier, inc=1, device_id={"dp": d, "seq": p}, device_id_type=MESH)

    barrier = pltpu.get_barrier_semaphore()

    @pl.loop(1, n)
    def _(k):
        greet(lax.rem(me + k, n), doc)

    greet(me, other)

    @pl.loop(0, jobs)
    def _(slot):
        greet(chunk(slot), other)

    for h in range(2):
        greet(owner(h, me)[0], other)
    pl.semaphore_wait(barrier, n + 2 + jobs)

    def u_copy(h, j):
        p, slot = owner(h, j)
        return p, remote(up.at[:, at(j), :], U.at[slot, me], su.at[h, j], ru.at[slot, me], p)

    def direct(h, j):
        return (h == half) | jnp.logical_not(outer) | (lax.div(j, plane) < outer_jobs)

    def f_copy(h):
        p, slot = owner(h, me)
        return p, remote(cf, cfs.at[slot], sk.at[h], rk.at[slot], p)

    @pl.loop(0, n)
    def _(step):
        j = turn(step)
        for far in (1, 0):
            h = 1 - half if far else half
            p, copy = u_copy(h, j)

            @pl.when((p != me) & direct(h, j))
            def _():
                copy.start()

    for h in range(2):
        p, copy = f_copy(h)

        @pl.when(p != me)
        def _():
            copy.start()

        @pl.when(p == me)
        def _():
            cfs[owner(h, me)[1]] = cf[...]

    @pl.loop(0, jobs)
    def _(slot):
        U[slot, me] = up[:, at(chunk(slot)), :]

    for r in range(rows):
        for q in range(0, D, 256):
            mloc[r, :, q:q + 256] = dot(rf[r], tok[r, :, q:q + 256]).astype(BF16)

    def wait_u_sends():
        @pl.loop(0, n)
        def _(j):
            for h in range(2):
                p, copy = u_copy(h, j)

                @pl.when((p != me) & direct(h, j))
                def _():
                    copy.wait_send()

    @pl.when(outer)
    def _():
        wait_u_sends()

    def m_copy(j):
        p, slot = owner(half, j)
        src = me - base
        return p, remote(mloc.at[:, at(j), :], M.at[slot, src], sm.at[j], rm.at[slot, src], p)

    @pl.loop(0, n)
    def _(step):
        p, copy = m_copy(turn(step))

        @pl.when(p != me)
        def _():
            copy.start()

    @pl.loop(0, jobs)
    def _(slot):
        M[slot, me - base] = mloc[:, at(chunk(slot)), :]

    def u_arrival(slot, src):
        return remote(U.at[slot, src], U.at[slot, src], sf.at[slot, lax.rem(src, plane)],
                      ru.at[slot, src], n - 1 - me + 2 * lax.rem(me, plane) - plane + 1)

    edge = half * (layers - 1) * plane

    @pl.when(jnp.logical_not(outer))
    def _():
        @pl.loop(0, inner_jobs)
        def _(slot):
            @pl.loop(0, plane)
            def _(q):
                copy = u_arrival(slot, edge + q)
                copy.wait_recv()
                copy.start()

    def iota(shape, dim):
        return lax.broadcasted_iota(jnp.int32, shape, dim)

    def ones(mask):
        return mask.astype(F32).astype(BF16)

    i, j = iota((full, full), 0), iota((full, full), 1)
    perm = ones(((i >> lr) == (j & (cols - 1))) & ((i & (R - 1)) == (j >> lc)))
    same = (iota((part_rows, full), 0) & (cols - 1)) == (iota((part_rows, full), 1) & (cols - 1))
    spread = ones((iota((part_rows, R), 0) >> lc) + half * (R // 2) == iota((part_rows, R), 1))
    gather = ones((iota((part_rows, R // 2), 0) >> lc) == iota((part_rows, R // 2), 1))

    def b_copy(slot, q):
        j = chunk(slot)
        return base + q, remote(bloc.at[slot, q], B.at[j], sb.at[slot, q], rb.at[j], base + q)

    def back(slot):
        @pl.when(slot < jobs)
        def _():
            j = chunk(slot)

            @pl.when((j != me))
            def _():
                remote(cf, cfs.at[slot], sk.at[0], rk.at[slot], lax.rem(me + 1, n)).wait_recv()

            turned = dot(cfs[slot], perm, 0, 0).astype(BF16)
            kmat = jnp.where(same, dot(spread, turned), 0.0).astype(BF16)

            @pl.loop(0, n)
            def _(src):
                handed = jnp.logical_not(outer) & (src >= edge) & (src < edge + plane)

                @pl.when((src != me) & jnp.logical_not(handed))
                def _():
                    u_arrival(slot, src).wait_recv()

            for q in range(0, D, 256):
                flat = U[slot, :, :, :, q:q + 256].reshape(full, 256)
                bloc[slot, :, :, :, q:q + 256] = dot(kmat, flat).astype(BF16).reshape(
                    half_n, rows, cols, 256)

            @pl.loop(0, half_n)
            def _(step):
                p, copy = b_copy(slot, lax.rem(me + step, half_n))

                @pl.when(p != me)
                def _():
                    copy.start()

            B[j] = bloc[slot, me - base]

    def s_copy(slot, d):
        return remote(pcol.at[slot], pcolr.at[half, doc], sc.at[slot, d], rc.at[half, doc],
                      chunk(slot), d)

    def here(slot, d):
        return (chunk(slot) == me) & (doc == d)

    def column(slot):
        @pl.when(slot < jobs)
        def _():
            @pl.loop(0, half_n)
            def _(src):
                @pl.when(base + src != me)
                def _():
                    remote(mloc.at[:, at(0), :], M.at[slot, src], sm.at[0], rm.at[slot, src],
                           lax.rem(me + 1, n)).wait_recv()

            pairs = dot(M[slot].reshape(part_rows, D), U[slot].reshape(full, D), 1, 1)
            pairs = jnp.where(same, pairs, 0.0)
            high = pairs.astype(BF16)
            low = pairs - high.astype(F32)
            mid = low.astype(BF16)
            rest = (low - mid.astype(F32)).astype(BF16)
            pcol[slot] = dot(gather, high, 0, 0) + dot(gather, mid, 0, 0) + dot(gather, rest, 0, 0)
            for d in range(2):
                @pl.when(jnp.logical_not(here(slot, d)))
                def _():
                    s_copy(slot, d).start()

                @pl.when(here(slot, d))
                def _():
                    pcolr[half, doc] = pcol[slot]

    def row_copy(k):
        part = at(k, plane * cols)
        return remote(prow.at[:, part, :], precv.at[:, part, :], sr.at[k], rr.at[k], me, other)

    def row(k):
        @pl.loop(0, plane)
        def _(q):
            j = k * plane + q
            p, _slot = owner(half, j)

            @pl.when(p != me)
            def _():
                remote(bloc.at[0, 0], B.at[j], sb.at[0, 0], rb.at[j], p).wait_recv()

        part = at(k, plane * cols)
        for r in range(rows):
            block = B[k * plane:(k + 1) * plane, r].reshape(plane * cols, D)
            prow[r, part, :] = dot(block, tok[r], 1, 1).astype(BF16)
        row_copy(k).start()

    back(0)
    back(1)
    row(0)
    back(2)
    row(1)
    column(0)
    column(1)
    column(2)
    row(2)
    row(3)

    for h in range(2):
        for d in range(2):
            p, _slot = owner(h, me)

            @pl.when(jnp.logical_not((p == me) & (doc == d)))
            def _():
                remote(pcol.at[0], pcolr.at[h, d], sc.at[0, 0], rc.at[h, d],
                       lax.rem(me + 1, n)).wait_recv()

    total = jnp.concatenate([pcolr[0, 0] + pcolr[0, 1], pcolr[1, 0] + pcolr[1, 1]], axis=0)
    gcol[...] = dot(perm, total.astype(BF16), 1, 1).astype(BF16)

    for k in range(layers):
        row_copy(k).wait()
        part = pl.ds(k * plane * cols, plane * cols)
        grow[:, part, :] = (prow[:, part, :].astype(F32) + precv[:, part, :].astype(F32)).astype(BF16)

    @pl.when(jnp.logical_not(outer))
    def _():
        wait_u_sends()

        @pl.loop(0, inner_jobs)
        def _(slot):
            @pl.loop(0, plane)
            def _(q):
                u_arrival(slot, edge + q).wait_send()

    for h in range(2):
        p, copy = f_copy(h)

        @pl.when(p != me)
        def _():
            copy.wait_send()

    @pl.loop(0, n)
    def _(j):
        p, copy = m_copy(j)

        @pl.when(p != me)
        def _():
            copy.wait_send()

    @pl.loop(0, jobs)
    def _(slot):
        @pl.loop(0, half_n)
        def _(q):
            p, copy = b_copy(slot, q)

            @pl.when(p != me)
            def _():
                copy.wait_send()

        for d in range(2):
            @pl.when(jnp.logical_not(here(slot, d)))
            def _():
                s_copy(slot, d).wait_send()


def fused_shards(n, tokens, upstream, row_factor, column_factor):
    _, rows, C, D = tokens.shape
    cols, R = C // n, rows * n
    full = R * cols
    outer_jobs, slots = 1, 3
    vmem = pl.BlockSpec(memory_space=pltpu.VMEM)
    dma = pltpu.SemaphoreType.DMA
    grow, gcol = pl.pallas_call(
        functools.partial(kernel, n, outer_jobs),
        out_shape=(
            jax.ShapeDtypeStruct((rows, C, C), BF16),
            jax.ShapeDtypeStruct((full, R), BF16),
        ),
        in_specs=[vmem] * 4,
        out_specs=(vmem, vmem),
        scratch_shapes=[
            pltpu.VMEM((slots, n, rows, cols, D), BF16),
            pltpu.VMEM((slots, n // 2, rows, cols, D), BF16),
            pltpu.VMEM((rows, C, D), BF16),
            pltpu.VMEM((slots, n // 2, rows, cols, D), BF16),
            pltpu.VMEM((n, rows, cols, D), BF16),
            pltpu.VMEM((slots, full, R), BF16),
            pltpu.VMEM((rows, C, C), BF16),
            pltpu.VMEM((rows, C, C), BF16),
            pltpu.VMEM((slots, R // 2, full), F32),
            pltpu.VMEM((2, 2, R // 2, full), F32),
            dma((2, n)), dma((slots, n)), dma((slots, n // 4)),
            dma((n,)), dma((slots, n // 2)),
            dma((slots, n // 2)), dma((n,)),
            dma((2,)), dma((slots,)),
            dma((4,)), dma((4,)),
            dma((slots, 2)), dma((2, 2)),
        ],
        compiler_params=pltpu.CompilerParams(
            collective_id=0, has_side_effects=True, vmem_limit_bytes=48 << 20
        ),
    )(tokens[0], upstream[0], row_factor, column_factor.reshape(full, R))
    return grow, gcol.reshape(cols, R, R)


def shards(n, m, tokens, upstream, row_factor, column_factor):
    docs, rows, C, D = tokens.shape
    cols, R = C // n, rows * n
    power = R & (R - 1) == 0 and cols & (cols - 1) == 0
    if m == 2 and docs == 1 and n == 16 and cols % 16 == 0 and D % 256 == 0 and power:
        return fused_shards(n, tokens, upstream, row_factor, column_factor)
    return plain_shards(tokens, upstream, row_factor, column_factor)


def solution(mesh):
    placed = (
        P("dp", "seq", None, None),
        P("dp", "seq", None, None),
        P("seq", None, None),
        P("seq", None, None),
    )
    return jax.shard_map(
        functools.partial(shards, mesh.shape["seq"], mesh.shape["dp"]),
        mesh=mesh,
        in_specs=placed,
        out_specs=(P("seq", None, None), P("seq", None, None)),
        check_vma=False,
    )
```
